512 devices in a mesh: gx: 32 (over z, x), gy: 16 (over y, core).
Axes of the slice: x: 4, y: 8, z: 8, core: 2. Of those that a mesh axis runs over, the one named last changes fastest.
Arguments:
- state: float32 [12, 96, 131072], P(None, None, ('gx', 'gy')), may hold values from -6 to 6
- events: int32 [8, 131072], P(None, ('gx', 'gy')), may hold values 0 or 1
- event_embed: float32 [96], replicated, may hold values from -4 to 4
- gains: float32 [3, 96], replicated, may hold values from 0.5 to 1.5
- taps_t: float32 [96, 9], replicated, may hold values from -2 to 2
- taps_y: float32 [96, 33], replicated, may hold values from -1 to 1
- taps_x: float32 [96, 33], replicated, may hold values from -1 to 1
- mixers: float32 [3, 2, 96, 96], replicated, may hold values from -0.625 to 0.625
Outputs:
- result: float32 [12, 96, 131072], P(None, None, ('gx', 'gy'))
The draws below stay inside these ranges and needn't reach their ends.
All inputs are finite; a program needn't handle non-finite values. No bound on the sum of `events` on one device may be relied on, other than what follows from the above.
Results may differ from the reference program's by a relative error of at most 0.0003.
Values sent between devices are 32-bit elements; how exact they have to be, the bound alone decides.
No kernel may reach another device: no remote copies, remote signals or barrier semaphores. Data moves between devices by JAX's collectives and lax.ppermute only.
A program may use at most 128 MiB of HBM per device.

```python
import jax
import jax.numpy as jnp
from jax import lax

C = 96
ROUNDS = 12
HIST = 8
KT = 9
KS = 33
X_DEV = 16
Y_DEV = 16
NX = 512
NY = 256
SITES = 131072
N_GX = 32
N_GY = 16


def place_ends(drawn, key, smallest, largest):
    shape = drawn.shape
    place = [jax.random.randint(jax.random.fold_in(key, axis), (), 0, shape[axis]) for axis in range(len(shape))]
    drawn = drawn.at[tuple(place)].set(smallest)
    longest = shape.index(max(shape))
    place[longest] = (place[longest] + 1) % shape[longest]
    return drawn.at[tuple(place)].set(largest)


def shard_levels(rng, extent, pieces, low, largest):
    factor_of = 1.0
    for axis_at, blocks in pieces:
        draws = jax.random.uniform(jax.random.fold_in(jax.random.fold_in(rng, 6), axis_at), (blocks,), jnp.float32, low / len(pieces), largest / len(pieces))
        factor_of = factor_of * jnp.repeat(jnp.exp(draws), extent[axis_at] // blocks).reshape((-1,) + (1,) * (len(extent) - 1 - axis_at))
    return factor_of


def centred(key, dims, spread, most, cuts=(), kind=jnp.bfloat16):
    values = spread * jax.random.normal(key, dims, jnp.float32)
    if cuts:
        values = values * shard_levels(key, dims, cuts, -0.22, 0.18)
    return jnp.clip(values, -most, most).astype(kind)


def setup_inputs(seed: int = 0) -> dict:
    key_of = jax.random.split(jax.random.key(seed), 9)
    state = centred(key_of[0], (ROUNDS, C, SITES), 1.0, 6.0, ((2, 512),), jnp.float32)
    events = place_ends((jax.random.randint(key_of[1], (HIST, SITES), 0, 2) < 1).astype(jnp.int32), jax.random.fold_in(key_of[1], 1), 0, 1)
    event_embed = centred(key_of[2], (C,), 1.0, 4.0, (), jnp.float32)
    gains = jnp.clip(1.0 + 0.1 * jax.random.normal(key_of[3], (3, C), jnp.float32), 0.5, 1.5)
    taps_t = centred(key_of[4], (C, KT), KT ** -0.5, 2.0, (), jnp.float32)
    taps_y = centred(key_of[5], (C, KS), KS ** -0.5, 1.0, (), jnp.float32)
    taps_x = centred(key_of[6], (C, KS), KS ** -0.5, 1.0, (), jnp.float32)
    mixers = centred(key_of[7], (3, 2, C, C), C ** -0.5, 0.625, (), jnp.float32)
    return dict(state=state, events=events, event_embed=event_embed, gains=gains, taps_t=taps_t, taps_y=taps_y, taps_x=taps_x, mixers=mixers)


def to_lattice(flat):
    lead = flat.shape[:-1]
    grid = flat.reshape(lead + (N_GX, N_GY, X_DEV, Y_DEV))
    nlead = len(lead)
    order = tuple(range(nlead)) + (nlead, nlead + 2, nlead + 1, nlead + 3)
    return jnp.transpose(grid, order).reshape(lead + (NX, NY))

def to_blocks(field):
    lead = field.shape[:-2]
    grid = field.reshape(lead + (N_GX, X_DEV, N_GY, Y_DEV))
    nlead = len(lead)
    order = tuple(range(nlead)) + (nlead, nlead + 2, nlead + 1, nlead + 3)
    return jnp.transpose(grid, order).reshape(lead + (NX * NY,))

def normed(field, gain):
    meansq = lax.optimization_barrier(jnp.mean(field * field, axis=0, keepdims=True))
    return field * lax.rsqrt(meansq + 1e-06) * gain[:, None, None]

def mixed(field, conv, weights):
    value = jnp.einsum('oc,cxy->oxy', weights[0], conv, precision=lax.Precision.HIGHEST)
    gate = jnp.einsum('oc,cxy->oxy', weights[1], conv, precision=lax.Precision.HIGHEST)
    return field + value * jax.nn.sigmoid(gate)

def spatial(field, gain, taps, weights, axis):
    source = normed(field, gain)
    half = taps.shape[1] // 2
    width = field.shape[axis]
    pads = [(0, 0), (0, 0), (0, 0)]
    pads[axis] = (half, half)
    padded = jnp.pad(source, pads)
    conv = jnp.zeros_like(field)
    for k in range(taps.shape[1]):
        piece = lax.slice_in_dim(padded, k, k + width, axis=axis)
        conv = conv + taps[:, k][:, None, None] * piece
    return mixed(field, conv, weights)

def reference(state, events, event_embed, gains, taps_t, taps_y, taps_x, mixers):
    grid_state = to_lattice(state)
    grid_events = to_lattice(events)

    def time_round(r):
        field = lax.dynamic_index_in_dim(grid_state, r, 0, keepdims=False)
        conv = jnp.zeros_like(field)
        for k in range(KT):
            s = r + k - (KT - 1)
            srow = jnp.clip(s, 0, ROUNDS - 1).astype(jnp.int32)
            hrow = jnp.clip(s + HIST, 0, HIST - 1).astype(jnp.int32)
            now = normed(lax.dynamic_index_in_dim(grid_state, srow, 0, keepdims=False), gains[0])
            ev = lax.dynamic_index_in_dim(grid_events, hrow, 0, keepdims=False)
            past = event_embed[:, None, None] * (2.0 * ev.astype(jnp.float32) - 1.0)[None]
            conv = conv + taps_t[:, k][:, None, None] * jnp.where(s < 0, past, now)
        return mixed(field, conv, mixers[0])
    h1 = lax.map(time_round, jnp.arange(ROUNDS, dtype=jnp.int32))
    h2 = lax.map(lambda f: spatial(f, gains[1], taps_y, mixers[1], 2), h1)
    h3 = lax.map(lambda f: spatial(f, gains[2], taps_x, mixers[2], 1), h2)
    return to_blocks(h3)
```

```python
import functools

import jax
import jax.numpy as jnp
import numpy as np
from jax import lax
from jax.experimental import pallas as pl
from jax.experimental.pallas import tpu as pltpu
from jax.sharding import PartitionSpec as P

C = 96
ROUNDS = 12
SITES = 256
LANES = 128
HALF = 16
HIST = 8
KT = 9
CHUNK = 6
VMEM = 20 * 1024 * 1024


def lane_orders():
    x, y = np.divmod(np.arange(SITES), 16)
    native = x * 16 + y
    along_y = (x // 8) * 128 + y * 8 + x % 8
    along_x = (y // 8) * 128 + x * 8 + y % 8
    return native, along_y, along_x


def moving(source, target):
    matrix = np.zeros((SITES, SITES), np.float32)
    matrix[source, target] = 1.0
    return jnp.asarray(np.concatenate([matrix, matrix], axis=0), jnp.bfloat16)


def halves(value):
    high = value.astype(jnp.bfloat16)
    low = (value - high.astype(jnp.float32)).astype(jnp.bfloat16)
    return high, low


def dot(a, b):
    return jnp.dot(a, b, preferred_element_type=jnp.float32)


def columns(*rows):
    have = sum(r.shape[0] for r in rows)
    pad = -have % 8
    parts = list(rows) + ([jnp.zeros((pad, C), jnp.float32)] if pad else [])
    stacked = jnp.concatenate(parts, axis=0) if len(parts) > 1 else parts[0]
    stacked = jnp.concatenate([stacked, jnp.zeros((have + pad, LANES - C), jnp.float32)], axis=1)
    return jnp.transpose(stacked)


def spread(column, lanes):
    return jnp.broadcast_to(column, (column.shape[0], lanes))


def normed(field, gain):
    meansq = jnp.sum(field * field, axis=0, keepdims=True) * (1.0 / C)
    return field * lax.rsqrt(meansq + 1e-06) * gain


def tail(count, first, field, conv, mixers, matrix, gain, parts, field_out, next_out, sent=None):
    weights = jnp.concatenate([mixers[0, 0], mixers[0, 1]], axis=0) * 0.5
    weights_high, weights_low = halves(weights)
    weights_twice = jnp.concatenate([weights_high, weights_high], axis=1)
    for r in range(count):
        high, low = halves(conv[r])
        both = dot(weights_twice, jnp.concatenate([high, low], axis=0)) + dot(weights_low, high)
        value = both[:C]
        mixed = field[first + r] + value + value * jnp.tanh(both[C:])
        high, low = halves(mixed)
        rows = slice(r * C, (r + 1) * C)
        parts[rows, :SITES] = high
        parts[rows, SITES:] = low
    moved = dot(parts[...], matrix[...])
    for r in range(count):
        here = moved[r * C : (r + 1) * C]
        field_out[r] = here
        if sent is not None:
            sent(r)
        if next_out is not None:
            next_out[r] = normed(here, gain)


def rounds_kernel(
    first, state_in, events_in, embed_in, gains_in, taps_in, mixers_in, matrix_in, field_out, next_out, *work
):
    ext, state, events, embed, gains, taps, mixers, matrix, conv, parts, sems = work
    last = state.shape[0]
    count = last - first
    small = [
        (gains_in, gains),
        (taps_in, taps),
        (embed_in, embed),
        (events_in, events),
        (mixers_in.at[0:1], mixers),
        (matrix_in, matrix),
    ]
    rounds = range(max(0, first - HIST), last)
    copies = [pltpu.make_async_copy(a, b, sems.at[last + n]) for n, (a, b) in enumerate(small)]
    loads = {r: pltpu.make_async_copy(state_in.at[r], state.at[r], sems.at[r]) for r in rounds}
    for copy in copies[:4] + list(loads.values()) + copies[4:]:
        copy.start()
    for copy in copies[:4]:
        copy.wait()
    cols = columns(taps[...], gains[...], embed[...])[:C]
    gain_now = spread(cols[:, KT : KT + 1], SITES)
    gain_next = spread(cols[:, KT + 1 : KT + 2], SITES)
    embed_here = spread(cols[:, KT + 3 : KT + 4], SITES)
    for s in range(first, HIST):
        past = 2.0 * events[s : s + 1, :].astype(jnp.float32) - 1.0
        ext[s] = embed_here * past
    for r in rounds:
        loads[r].wait()
        ext[HIST + r] = normed(state[r], gain_now)
    for i in range(C // 8):
        rows = slice(i * 8, (i + 1) * 8)
        tap = [spread(cols[rows, k : k + 1], LANES) for k in range(KT)]
        for half in range(2):
            lanes = slice(half * LANES, (half + 1) * LANES)
            seen = [ext[first + s, rows, lanes] for s in range(count + KT - 1)]
            for r in range(count):
                total = tap[0] * seen[r]
                for k in range(1, KT):
                    total = total + tap[k] * seen[r + k]
                conv[r, rows, lanes] = total
    for copy in copies[4:]:
        copy.wait()
    tail(count, first, state, conv, mixers, matrix, gain_next, parts, field_out, next_out)


def tables_kernel(taps, own, far):
    lane_place = lax.broadcasted_iota(jnp.int32, (8, LANES), 1) // 8
    cols = columns(taps[...])[:C]
    for i in range(C // 8):
        rows = slice(i * 8, (i + 1) * 8)
        tap = [spread(cols[rows, k : k + 1], LANES) for k in range(2 * HALF + 1)]
        for d in range(HALF):
            keep = turned_place(lane_place, d) >= d
            own[d, rows, :] = jnp.where(keep, tap[d + HALF], tap[d])
            far[d, rows, :] = jnp.where(keep, tap[d], tap[d + HALF])
        far[HALF, rows, :] = tap[2 * HALF]


def turned_place(lane_place, d):
    return lax.rem(lane_place + 1, HALF) if d % 2 else lane_place


def lattice_kernel(axis, ends, part, *refs):
    field, own, odd, even, gains, tap_own, tap_far, mixers, matrix = refs[:9]
    if ends:
        result, conv, parts, sems = refs[-4:]
    else:
        field_out, next_out, conv, parts = refs[9:]
        gain = spread(columns(gains[...])[:C, 2:3], SITES)
    count = field.shape[0]
    lane_place = lax.broadcasted_iota(jnp.int32, (8, LANES), 1) // 8
    first_of_pair = lax.rem(lax.axis_index(axis), 2) == 0

    def conv_tile(i, carry):
        rows = pl.ds(pl.multiple_of(i * 8, 8), 8)
        for r0 in range(0, count, 2):
            spots = [
                (r, slice(half * LANES, (half + 1) * LANES)) for r in range(r0, r0 + 2) for half in range(2)
            ]
            here = [own[r, rows, lanes] for r, lanes in spots]
            one = [even[r, rows, lanes] for r, lanes in spots]
            two = [odd[r, rows, lanes] for r, lanes in spots]
            low = [jnp.where(first_of_pair, b, a) for a, b in zip(one, two)]
            high = [jnp.where(first_of_pair, a, b) for a, b in zip(one, two)]
            turned = [[pltpu.roll(v, LANES - 8, 1) for v in vs] for vs in (here, low, high)]
            sides = ((here, low, high), turned)
            totals = [tap_far[HALF, rows, :] * high[n] for n in range(len(spots))]
            for d in range(0, HALF, 2):
                sums = [None] * len(spots)
                for e in (d, d + 1):
                    near = tap_own[e, rows, :]
                    far = tap_far[e, rows, :]
                    keep = turned_place(lane_place, e) >= e
                    mine, under, over = sides[e - d]
                    for n in range(len(spots)):
                        other = jnp.where(keep, under[n], over[n]) if e else under[n]
                        piece = near * mine[n] + far * other
                        sums[n] = piece if e == d else sums[n] + piece
                for n in range(len(spots)):
                    totals[n] = totals[n] + (pltpu.roll(sums[n], LANES - 8 * d, 1) if d else sums[n])
            for n, (r, lanes) in enumerate(spots):
                conv[r, rows, lanes] = totals[n]
        return carry

    lax.fori_loop(0, C // 8, conv_tile, 0)
    if not ends:
        tail(count, 0, field, conv, mixers, matrix, gain, parts, field_out, next_out)
        return

    copies = [
        pltpu.make_async_copy(conv.at[r], result.at[part * CHUNK + r], sems.at[r]) for r in range(count)
    ]
    tail(count, 0, field, conv, mixers, matrix, None, parts, conv, None, lambda r: copies[r].start())
    for copy in copies:
        copy.wait()


def whole(shape):
    return pl.BlockSpec(shape, lambda *_: (0,) * len(shape))


def picked(shape, place):
    return pl.BlockSpec((1,) + shape[1:], lambda *_: (place,) + (0,) * (len(shape) - 1))


def cost(flops):
    return pl.CostEstimate(flops=flops, bytes_accessed=100_000, transcendentals=0)


PARAMS = pltpu.CompilerParams(vmem_limit_bytes=VMEM)
BLOCK = (CHUNK, C, SITES)
FULL = (ROUNDS, C, SITES)
WORK = [pltpu.VMEM(BLOCK, jnp.float32), pltpu.VMEM((CHUNK * C, 2 * SITES), jnp.bfloat16)]


def rounds_pass(part, inputs):
    state, events, embed, gains, taps, mixers, matrix = inputs
    first = part * CHUNK
    last = first + CHUNK
    outs = [BLOCK, BLOCK]
    return pl.pallas_call(
        functools.partial(rounds_kernel, first),
        grid=(1,),
        in_specs=[pl.BlockSpec(memory_space=pltpu.HBM)] * 7,
        out_specs=[whole(o) for o in outs],
        out_shape=[jax.ShapeDtypeStruct(o, jnp.float32) for o in outs],
        scratch_shapes=[
            pltpu.VMEM((HIST + last, C, SITES), jnp.float32),
            pltpu.VMEM((last, C, SITES), jnp.float32),
            pltpu.VMEM(events.shape, jnp.int32),
            pltpu.VMEM(embed.shape, jnp.float32),
            pltpu.VMEM(gains.shape, jnp.float32),
            pltpu.VMEM(taps.shape, jnp.float32),
            pltpu.VMEM((1,) + mixers.shape[1:], jnp.float32),
            pltpu.VMEM(matrix.shape, jnp.bfloat16),
        ]
        + WORK
        + [pltpu.SemaphoreType.DMA((last + 6,))],
        compiler_params=PARAMS,
        cost_estimate=cost(20_000_000),
    )(*inputs)


def tap_tables(taps):
    outs = [jax.ShapeDtypeStruct((HALF + n, C, LANES), jnp.float32) for n in range(2)]
    return pl.pallas_call(
        tables_kernel,
        grid=(1,),
        in_specs=[whole(taps.shape)],
        out_specs=[whole(o.shape) for o in outs],
        out_shape=outs,
        compiler_params=PARAMS,
        cost_estimate=cost(1_000_000),
    )(taps)


def lattice_pass(axis, field, own, sides, gains, table, mixers, matrix):
    args = (field, own, *sides, gains, *table, mixers, matrix)
    return pl.pallas_call(
        functools.partial(lattice_kernel, axis, False, 0),
        grid=(1,),
        in_specs=[whole(a.shape) for a in args[:-2]] + [picked(mixers.shape, 1), whole(matrix.shape)],
        out_specs=[whole(BLOCK)] * 2,
        out_shape=[jax.ShapeDtypeStruct(BLOCK, jnp.float32)] * 2,
        scratch_shapes=WORK,
        compiler_params=PARAMS,
        cost_estimate=cost(1_200_000_000),
    )(*args)


def last_pass(axis, part, result, field, own, sides, gains, table, mixers, matrix):
    args = (field, own, *sides, gains, *table, mixers, matrix)
    specs = [whole(a.shape) for a in args[:-2]] + [picked(mixers.shape, 2), whole(matrix.shape)]
    aliases = {}
    if result is not None:
        aliases = {len(args): 0}
        args = args + (result,)
        specs = specs + [pl.BlockSpec(memory_space=pl.ANY)]
    return pl.pallas_call(
        functools.partial(lattice_kernel, axis, True, part),
        grid=(1,),
        in_specs=specs,
        out_specs=pl.BlockSpec(memory_space=pl.ANY),
        out_shape=jax.ShapeDtypeStruct(FULL, jnp.float32),
        scratch_shapes=WORK + [pltpu.SemaphoreType.DMA((CHUNK,))],
        input_output_aliases=aliases,
        compiler_params=PARAMS,
        cost_estimate=cost(1_200_000_000),
    )(*args)


def swap(own, axis, start):
    count = lax.axis_size(axis)
    pairs = [p for i in range(start, count - 1, 2) for p in ((i, i + 1), (i + 1, i))]
    return lax.ppermute(own, axis, pairs)


def local(state, events, event_embed, gains, taps_t, taps_y, taps_x, mixers):
    native, along_y, along_x = lane_orders()
    to_y = moving(native, along_y)
    to_x = moving(along_y, along_x)
    back = moving(along_x, native)
    inputs = [
        pltpu.with_memory_space_constraint(a, pltpu.HBM)
        for a in (state, events, event_embed[None, :], gains, taps_t.T, mixers, to_y)
    ]

    field_a, own_a = rounds_pass(0, inputs)
    odd_a = swap(own_a, "gy", 1)
    even_a = swap(own_a, "gy", 0)
    field_b, own_b = rounds_pass(1, inputs)
    even_b = swap(own_b, "gy", 0)
    taps_y, own_b = lax.optimization_barrier((taps_y, own_b))
    table_y = tap_tables(taps_y.T)
    own_b, table_y = lax.optimization_barrier((own_b, table_y))
    odd_b = swap(own_b, "gy", 1)
    field_a, own_a = lattice_pass("gy", field_a, own_a, (odd_a, even_a), gains, table_y, mixers, to_x)
    even_a = swap(own_a, "gx", 0)
    odd_a = swap(own_a, "gx", 1)
    field_b, own_b = lattice_pass("gy", field_b, own_b, (odd_b, even_b), gains, table_y, mixers, to_x)
    even_b = swap(own_b, "gx", 0)
    odd_b = swap(own_b, "gx", 1)
    taps_x, own_b = lax.optimization_barrier((taps_x, own_b))
    table_x = tap_tables(taps_x.T)
    result = last_pass("gx", 0, None, field_a, own_a, (odd_a, even_a), gains, table_x, mixers, back)
    return last_pass("gx", 1, result, field_b, own_b, (odd_b, even_b), gains, table_x, mixers, back)


def solution(mesh):
    placed = (P(None, None, ("gx", "gy")), P(None, ("gx", "gy")), P(), P(), P(), P(), P(), P())
    return jax.shard_map(
        local, mesh=mesh, in_specs=placed, out_specs=P(None, None, ("gx", "gy")), check_vma=False
    )
```

```python
import functools

import jax
import jax.numpy as jnp
import numpy as np
from jax import lax
from jax.experimental import pallas as pl
from jax.experimental.pallas import tpu as pltpu
from jax.sharding import PartitionSpec as P

C = 96
ROUNDS = 12
SITES = 256
LANES = 128
HALF = 16
HIST = 8
KT = 9
CHUNK = 6
VMEM = 20 * 1024 * 1024


def lane_orders():
    x, y = np.divmod(np.arange(SITES), 16)
    native = x * 16 + y
    along_y = (x // 8) * 128 + y * 8 + x % 8
    along_x = (y // 8) * 128 + x * 8 + y % 8
    return native, along_y, along_x


def moving(source, target):
    matrix = np.zeros((SITES, SITES), np.float32)
    matrix[source, target] = 1.0
    return jnp.asarray(np.concatenate([matrix, matrix], axis=0), jnp.bfloat16)


def halves(value):
    high = value.astype(jnp.bfloat16)
    low = (value - high.astype(jnp.float32)).astype(jnp.bfloat16)
    return high, low


def dot(a, b):
    return jnp.dot(a, b, preferred_element_type=jnp.float32)


def columns(*rows):
    have = sum(r.shape[0] for r in rows)
    pad = -have % 8
    parts = list(rows) + ([jnp.zeros((pad, C), jnp.float32)] if pad else [])
    stacked = jnp.concatenate(parts, axis=0) if len(parts) > 1 else parts[0]
    stacked = jnp.concatenate([stacked, jnp.zeros((have + pad, LANES - C), jnp.float32)], axis=1)
    return jnp.transpose(stacked)


def spread(column, lanes):
    return jnp.broadcast_to(column, (column.shape[0], lanes))


def normed(field, gain):
    meansq = jnp.sum(field * field, axis=0, keepdims=True) * (1.0 / C)
    return field * lax.rsqrt(meansq + 1e-06) * gain


def tail(count, first, field, conv, mixers, matrix, gain, parts, field_out, next_out, sent=None):
    weights = jnp.concatenate([mixers[0, 0], mixers[0, 1]], axis=0) * 0.5
    weights_high, weights_low = halves(weights)
    weights_twice = jnp.concatenate([weights_high, weights_high], axis=1)
    for r in range(count):
        high, low = halves(conv[r])
        both = dot(weights_twice, jnp.concatenate([high, low], axis=0)) + dot(weights_low, high)
        value = both[:C]
        mixed = field[first + r] + value + value * jnp.tanh(both[C:])
        high, low = halves(mixed)
        rows = slice(r * C, (r + 1) * C)
        parts[rows, :SITES] = high
        parts[rows, SITES:] = low
    moved = dot(parts[...], matrix[...])
    for r in range(count):
        here = moved[r * C : (r + 1) * C]
        field_out[r] = here
        if sent is not None:
            sent(r)
        if next_out is not None:
            next_out[r] = normed(here, gain)


def rounds_kernel(
    first, state_in, events_in, embed_in, gains_in, taps_in, mixers_in, matrix_in, field_out, next_out, *work
):
    ext, state, events, embed, gains, taps, mixers, matrix, conv, parts, sems = work
    last = state.shape[0]
    count = last - first
    small = [
        (gains_in, gains),
        (taps_in, taps),
        (embed_in, embed),
        (events_in, events),
        (mixers_in.at[0:1], mixers),
        (matrix_in, matrix),
    ]
    rounds = range(max(0, first - HIST), last)
    copies = [pltpu.make_async_copy(a, b, sems.at[last + n]) for n, (a, b) in enumerate(small)]
    loads = {r: pltpu.make_async_copy(state_in.at[r], state.at[r], sems.at[r]) for r in rounds}
    for copy in copies[:4] + list(loads.values()) + copies[4:]:
        copy.start()
    for copy in copies[:4]:
        copy.wait()
    cols = columns(taps[...], gains[...], embed[...])[:C]
    gain_now = spread(cols[:, KT : KT + 1], SITES)
    gain_next = spread(cols[:, KT + 1 : KT + 2], SITES)
    embed_here = spread(cols[:, KT + 3 : KT + 4], SITES)
    for s in range(first, HIST):
        past = 2.0 * events[s : s + 1, :].astype(jnp.float32) - 1.0
        ext[s] = embed_here * past
    for r in rounds:
        loads[r].wait()
        ext[HIST + r] = normed(state[r], gain_now)
    for i in range(C // 8):
        rows = slice(i * 8, (i + 1) * 8)
        tap = [spread(cols[rows, k : k + 1], LANES) for k in range(KT)]
        for half in range(2):
            lanes = slice(half * LANES, (half + 1) * LANES)
            seen = [ext[first + s, rows, lanes] for s in range(count + KT - 1)]
            for r in range(count):
                total = tap[0] * seen[r]
                for k in range(1, KT):
                    total = total + tap[k] * seen[r + k]
                conv[r, rows, lanes] = total
    for copy in copies[4:]:
        copy.wait()
    tail(count, first, state, conv, mixers, matrix, gain_next, parts, field_out, next_out)


def tables_kernel(kinds, taps, *tables):
    lane_place = lax.broadcasted_iota(jnp.int32, (8, LANES), 1) // 8
    cols = columns(taps[...])[:C]
    for i in range(C // 8):
        rows = slice(i * 8, (i + 1) * 8)
        tap = [spread(cols[rows, k : k + 1], LANES) for k in range(2 * HALF + 1)]
        for kind, table in zip(kinds, tables):
            for d in range(HALF):
                keep = turned_place(lane_place, d) >= d
                if kind == "own":
                    table[d, rows, :] = jnp.where(keep, tap[d + HALF], tap[d])
                else:
                    table[d, rows, :] = jnp.where(keep, tap[d], tap[d + HALF])
            if kind == "far":
                table[HALF, rows, :] = tap[2 * HALF]


def turned_place(lane_place, d):
    return (lane_place + 1) & (HALF - 1) if d % 2 else lane_place


def lattice_kernel(axis, ends, part, *refs):
    field, own, odd, even, gains, tap_own, tap_far, mixers, matrix = refs[:9]
    if ends:
        result, conv, parts, sems = refs[-4:]
    else:
        field_out, next_out, conv, parts = refs[9:]
        gain = spread(columns(gains[...])[:C, 2:3], SITES)
    count = field.shape[0]
    lane_place = lax.broadcasted_iota(jnp.int32, (8, LANES), 1) // 8
    first_of_pair = lax.rem(lax.axis_index(axis), 2) == 0

    def conv_tile(i, carry):
        rows = pl.ds(pl.multiple_of(i * 8, 8), 8)
        for r0 in range(0, count, 2):
            spots = [
                (r, slice(half * LANES, (half + 1) * LANES)) for r in range(r0, r0 + 2) for half in range(2)
            ]
            here = [own[r, rows, lanes] for r, lanes in spots]
            one = [even[r, rows, lanes] for r, lanes in spots]
            two = [odd[r, rows, lanes] for r, lanes in spots]
            low = [jnp.where(first_of_pair, b, a) for a, b in zip(one, two)]
            high = [jnp.where(first_of_pair, a, b) for a, b in zip(one, two)]
            turned = [[pltpu.roll(v, LANES - 8, 1) for v in vs] for vs in (here, low, high)]
            sides = ((here, low, high), turned)
            totals = [tap_far[HALF, rows, :] * high[n] for n in range(len(spots))]
            for d in range(0, HALF, 2):
                sums = [None] * len(spots)
                for e in (d, d + 1):
                    near = tap_own[e, rows, :]
                    far = tap_far[e, rows, :]
                    keep = turned_place(lane_place, e) >= e
                    mine, under, over = sides[e - d]
                    for n in range(len(spots)):
                        other = jnp.where(keep, under[n], over[n]) if e else under[n]
                        piece = near * mine[n] + far * other
                        sums[n] = piece if e == d else sums[n] + piece
                for n in range(len(spots)):
                    totals[n] = totals[n] + (pltpu.roll(sums[n], LANES - 8 * d, 1) if d else sums[n])
            for n, (r, lanes) in enumerate(spots):
                conv[r, rows, lanes] = totals[n]
        return carry

    lax.fori_loop(0, C // 8, conv_tile, 0)
    if not ends:
        tail(count, 0, field, conv, mixers, matrix, gain, parts, field_out, next_out)
        return

    copies = [
        pltpu.make_async_copy(conv.at[r], result.at[part * CHUNK + r], sems.at[r]) for r in range(count)
    ]
    tail(count, 0, field, conv, mixers, matrix, None, parts, conv, None, lambda r: copies[r].start())
    for copy in copies:
        copy.wait()


def whole(shape):
    return pl.BlockSpec(shape, lambda *_: (0,) * len(shape))


def picked(shape, place):
    return pl.BlockSpec((1,) + shape[1:], lambda *_: (place,) + (0,) * (len(shape) - 1))


def cost(flops):
    return pl.CostEstimate(flops=flops, bytes_accessed=100_000, transcendentals=0)


PARAMS = pltpu.CompilerParams(vmem_limit_bytes=VMEM)
BLOCK = (CHUNK, C, SITES)
FULL = (ROUNDS, C, SITES)
WORK = [pltpu.VMEM(BLOCK, jnp.float32), pltpu.VMEM((CHUNK * C, 2 * SITES), jnp.bfloat16)]


def rounds_pass(part, inputs):
    state, events, embed, gains, taps, mixers, matrix = inputs
    first = part * CHUNK
    last = first + CHUNK
    outs = [BLOCK, BLOCK]
    return pl.pallas_call(
        functools.partial(rounds_kernel, first),
        grid=(1,),
        in_specs=[pl.BlockSpec(memory_space=pltpu.HBM)] * 7,
        out_specs=[whole(o) for o in outs],
        out_shape=[jax.ShapeDtypeStruct(o, jnp.float32) for o in outs],
        scratch_shapes=[
            pltpu.VMEM((HIST + last, C, SITES), jnp.float32),
            pltpu.VMEM((last, C, SITES), jnp.float32),
            pltpu.VMEM(events.shape, jnp.int32),
            pltpu.VMEM(embed.shape, jnp.float32),
            pltpu.VMEM(gains.shape, jnp.float32),
            pltpu.VMEM(taps.shape, jnp.float32),
            pltpu.VMEM((1,) + mixers.shape[1:], jnp.float32),
            pltpu.VMEM(matrix.shape, jnp.bfloat16),
        ]
        + WORK
        + [pltpu.SemaphoreType.DMA((last + 6,))],
        compiler_params=PARAMS,
        cost_estimate=cost(20_000_000),
    )(*inputs)


def tap_tables(kinds, taps, after):
    taps, after = lax.optimization_barrier((taps, after))
    outs = [jax.ShapeDtypeStruct((HALF + (kind == "far"), C, LANES), jnp.float32) for kind in kinds]
    return pl.pallas_call(
        functools.partial(tables_kernel, kinds),
        grid=(1,),
        in_specs=[whole(taps.shape[::-1])],
        out_specs=[whole(o.shape) for o in outs],
        out_shape=outs,
        compiler_params=PARAMS,
        cost_estimate=cost(1_000_000),
    )(taps.T)


def lattice_pass(axis, field, own, sides, gains, table, mixers, matrix):
    args = (field, own, *sides, gains, *table, mixers, matrix)
    return pl.pallas_call(
        functools.partial(lattice_kernel, axis, False, 0),
        grid=(1,),
        in_specs=[whole(a.shape) for a in args[:-2]] + [picked(mixers.shape, 1), whole(matrix.shape)],
        out_specs=[whole(BLOCK)] * 2,
        out_shape=[jax.ShapeDtypeStruct(BLOCK, jnp.float32)] * 2,
        scratch_shapes=WORK,
        compiler_params=PARAMS,
        cost_estimate=cost(1_200_000_000),
    )(*args)


def last_pass(axis, part, result, field, own, sides, gains, table, mixers, matrix):
    args = (field, own, *sides, gains, *table, mixers, matrix)
    specs = [whole(a.shape) for a in args[:-2]] + [picked(mixers.shape, 2), whole(matrix.shape)]
    aliases = {}
    if result is not None:
        aliases = {len(args): 0}
        args = args + (result,)
        specs = specs + [pl.BlockSpec(memory_space=pl.ANY)]
    return pl.pallas_call(
        functools.partial(lattice_kernel, axis, True, part),
        grid=(1,),
        in_specs=specs,
        out_specs=pl.BlockSpec(memory_space=pl.ANY),
        out_shape=jax.ShapeDtypeStruct(FULL, jnp.float32),
        scratch_shapes=WORK + [pltpu.SemaphoreType.DMA((CHUNK,))],
        input_output_aliases=aliases,
        compiler_params=PARAMS,
        cost_estimate=cost(1_200_000_000),
    )(*args)


def swap(own, axis, start):
    count = lax.axis_size(axis)
    pairs = [p for i in range(start, count - 1, 2) for p in ((i, i + 1), (i + 1, i))]
    return lax.ppermute(own, axis, pairs)


def local(state, events, event_embed, gains, taps_t, taps_y, taps_x, mixers):
    native, along_y, along_x = lane_orders()
    to_y = moving(native, along_y)
    to_x = moving(along_y, along_x)
    back = moving(along_x, native)
    inputs = [
        pltpu.with_memory_space_constraint(a, pltpu.HBM)
        for a in (state, events, event_embed[None, :], gains, taps_t.T, mixers, to_y)
    ]

    field_a, own_a = rounds_pass(0, inputs)
    odd_a = swap(own_a, "gy", 1)
    table_y, held = lax.optimization_barrier((tap_tables(("own", "far"), taps_y, own_a), own_a))
    even_a = swap(held, "gy", 0)
    field_b, own_b = rounds_pass(1, inputs)
    odd_b = swap(own_b, "gy", 1)
    even_b = swap(own_b, "gy", 0)
    field_a, own_a = lattice_pass("gy", field_a, own_a, (odd_a, even_a), gains, table_y, mixers, to_x)
    odd_a = swap(own_a, "gx", 1)
    near_x, held = lax.optimization_barrier((tap_tables(("own",), taps_x, own_a), own_a))
    even_a = swap(held, "gx", 0)
    field_b, own_b = lattice_pass("gy", field_b, own_b, (odd_b, even_b), gains, table_y, mixers, to_x)
    odd_b = swap(own_b, "gx", 1)
    far_x, held = lax.optimization_barrier((tap_tables(("far",), taps_x, own_b), own_b))
    even_b = swap(held, "gx", 0)
    table_x = (*near_x, *far_x)
    result = last_pass("gx", 0, None, field_a, own_a, (odd_a, even_a), gains, table_x, mixers, back)
    return last_pass("gx", 1, result, field_b, own_b, (odd_b, even_b), gains, table_x, mixers, back)


def solution(mesh):
    placed = (P(None, None, ("gx", "gy")), P(None, ("gx", "gy")), P(), P(), P(), P(), P(), P())
    return jax.shard_map(
        local, mesh=mesh, in_specs=placed, out_specs=P(None, None, ("gx", "gy")), check_vma=False
    )
```

```python
import functools

import jax
import jax.numpy as jnp
import numpy as np
from jax import lax
from jax.experimental import pallas as pl
from jax.experimental.pallas import tpu as pltpu
from jax.sharding import PartitionSpec as P

C = 96
ROUNDS = 12
SITES = 256
LANES = 128
HALF = 16
HIST = 8
KT = 9
CHUNK = 6
VMEM = 20 * 1024 * 1024


def lane_orders():
    x, y = np.divmod(np.arange(SITES), 16)
    native = x * 16 + y
    along_y = (x // 8) * 128 + y * 8 + x % 8
    along_x = (y // 8) * 128 + x * 8 + y % 8
    return native, along_y, along_x


def moving(source, target):
    matrix = np.zeros((SITES, SITES), np.float32)
    matrix[source, target] = 1.0
    return jnp.asarray(np.concatenate([matrix, matrix], axis=0), jnp.bfloat16)


def halves(value):
    high = value.astype(jnp.bfloat16)
    low = (value - high.astype(jnp.float32)).astype(jnp.bfloat16)
    return high, low


def dot(a, b):
    return jnp.dot(a, b, preferred_element_type=jnp.float32)


def columns(*rows):
    have = sum(r.shape[0] for r in rows)
    pad = -have % 8
    parts = list(rows) + ([jnp.zeros((pad, C), jnp.float32)] if pad else [])
    stacked = jnp.concatenate(parts, axis=0) if len(parts) > 1 else parts[0]
    stacked = jnp.concatenate([stacked, jnp.zeros((have + pad, LANES - C), jnp.float32)], axis=1)
    return jnp.transpose(stacked)


def spread(column, lanes):
    return jnp.broadcast_to(column, (column.shape[0], lanes))


def normed(field, gain):
    meansq = jnp.sum(field * field, axis=0, keepdims=True) * (1.0 / C)
    return field * lax.rsqrt(meansq + 1e-06) * gain


def tail(count, first, field, conv, mixers, matrix, gain, parts, field_out, next_out, sent=None):
    weights = jnp.concatenate([mixers[0, 0], mixers[0, 1]], axis=0) * 0.5
    weights_high, weights_low = halves(weights)
    weights_twice = jnp.concatenate([weights_high, weights_high], axis=1)
    for r in range(count):
        high, low = halves(conv[r])
        both = dot(weights_twice, jnp.concatenate([high, low], axis=0)) + dot(weights_low, high)
        value = both[:C]
        mixed = field[first + r] + value + value * jnp.tanh(both[C:])
        high, low = halves(mixed)
        rows = slice(r * C, (r + 1) * C)
        parts[rows, :SITES] = high
        parts[rows, SITES:] = low
    moved = dot(parts[...], matrix[...])
    for r in range(count):
        here = moved[r * C : (r + 1) * C]
        field_out[r] = here
        if sent is not None:
            sent(r)
        if next_out is not None:
            next_out[r] = normed(here, gain)


def rounds_kernel(
    first, state_in, events_in, embed_in, gains_in, taps_in, mixers_in, matrix_in, field_out, next_out, *work
):
    ext, state, events, embed, gains, taps, mixers, matrix, conv, parts, sems = work
    last = state.shape[0]
    count = last - first
    small = [
        (gains_in, gains),
        (taps_in, taps),
        (embed_in, embed),
        (events_in, events),
        (mixers_in.at[0:1], mixers),
        (matrix_in, matrix),
    ]
    rounds = range(max(0, first - HIST), last)
    copies = [pltpu.make_async_copy(a, b, sems.at[last + n]) for n, (a, b) in enumerate(small)]
    loads = {r: pltpu.make_async_copy(state_in.at[r], state.at[r], sems.at[r]) for r in rounds}
    for copy in copies[:4] + list(loads.values()) + copies[4:]:
        copy.start()
    for copy in copies[:4]:
        copy.wait()
    cols = columns(taps[...], gains[...], embed[...])[:C]
    gain_now = spread(cols[:, KT : KT + 1], SITES)
    gain_next = spread(cols[:, KT + 1 : KT + 2], SITES)
    embed_here = spread(cols[:, KT + 3 : KT + 4], SITES)
    for s in range(first, HIST):
        past = 2.0 * events[s : s + 1, :].astype(jnp.float32) - 1.0
        ext[s] = embed_here * past
    for r in rounds:
        loads[r].wait()
        ext[HIST + r] = normed(state[r], gain_now)
    for i in range(C // 8):
        rows = slice(i * 8, (i + 1) * 8)
        tap = [spread(cols[rows, k : k + 1], LANES) for k in range(KT)]
        for half in range(2):
            lanes = slice(half * LANES, (half + 1) * LANES)
            seen = [ext[first + s, rows, lanes] for s in range(count + KT - 1)]
            for r in range(count):
                total = tap[0] * seen[r]
                for k in range(1, KT):
                    total = total + tap[k] * seen[r + k]
                conv[r, rows, lanes] = total
    for copy in copies[4:]:
        copy.wait()
    tail(count, first, state, conv, mixers, matrix, gain_next, parts, field_out, next_out)


def tables_kernel(kinds, taps, *tables):
    lane_place = lax.broadcasted_iota(jnp.int32, (8, LANES), 1) // 8
    cols = columns(taps[...])[:C]
    for i in range(C // 8):
        rows = slice(i * 8, (i + 1) * 8)
        tap = [spread(cols[rows, k : k + 1], LANES) for k in range(2 * HALF + 1)]
        for kind, table in zip(kinds, tables):
            for d in range(HALF):
                keep = turned_place(lane_place, d) >= d
                if kind == "own":
                    table[d, rows, :] = jnp.where(keep, tap[d + HALF], tap[d])
                else:
                    table[d, rows, :] = jnp.where(keep, tap[d], tap[d + HALF])
            if kind == "far":
                table[HALF, rows, :] = tap[2 * HALF]


def turned_place(lane_place, d):
    return (lane_place + 1) & (HALF - 1) if d % 2 else lane_place


def lattice_kernel(axis, ends, part, *refs):
    field, own, odd, even, gains, tap_own, tap_far, mixers, matrix = refs[:9]
    if ends:
        result, conv, parts, sems = refs[-4:]
    else:
        field_out, next_out, conv, parts = refs[9:]
        gain = spread(columns(gains[...])[:C, 2:3], SITES)
    count = field.shape[0]
    lane_place = lax.broadcasted_iota(jnp.int32, (8, LANES), 1) // 8
    first_of_pair = lax.rem(lax.axis_index(axis), 2) == 0

    def conv_tile(i, carry):
        rows = pl.ds(pl.multiple_of(i * 8, 8), 8)
        for r0 in range(0, count, 2):
            spots = [
                (r, slice(half * LANES, (half + 1) * LANES)) for r in range(r0, r0 + 2) for half in range(2)
            ]
            here = [own[r, rows, lanes] for r, lanes in spots]
            one = [even[r, rows, lanes] for r, lanes in spots]
            two = [odd[r, rows, lanes] for r, lanes in spots]
            low = [jnp.where(first_of_pair, b, a) for a, b in zip(one, two)]
            high = [jnp.where(first_of_pair, a, b) for a, b in zip(one, two)]
            turned = [[pltpu.roll(v, LANES - 8, 1) for v in vs] for vs in (here, low, high)]
            sides = ((here, low, high), turned)
            totals = [tap_far[HALF, rows, :] * high[n] for n in range(len(spots))]
            for d in range(0, HALF, 2):
                sums = [None] * len(spots)
                for e in (d, d + 1):
                    near = tap_own[e, rows, :]
                    far = tap_far[e, rows, :]
                    keep = turned_place(lane_place, e) >= e
                    mine, under, over = sides[e - d]
                    for n in range(len(spots)):
                        other = jnp.where(keep, under[n], over[n]) if e else under[n]
                        piece = near * mine[n] + far * other
                        sums[n] = piece if e == d else sums[n] + piece
                for n in range(len(spots)):
                    totals[n] = totals[n] + (pltpu.roll(sums[n], LANES - 8 * d, 1) if d else sums[n])
            for n, (r, lanes) in enumerate(spots):
                conv[r, rows, lanes] = totals[n]
        return carry

    lax.fori_loop(0, C // 8, conv_tile, 0, unroll=3)
    if not ends:
        tail(count, 0, field, conv, mixers, matrix, gain, parts, field_out, next_out)
        return

    copies = [
        pltpu.make_async_copy(conv.at[r], result.at[part * CHUNK + r], sems.at[r]) for r in range(count)
    ]
    tail(count, 0, field, conv, mixers, matrix, None, parts, conv, None, lambda r: copies[r].start())
    for copy in copies:
        copy.wait()


def whole(shape):
    return pl.BlockSpec(shape, lambda *_: (0,) * len(shape))


def picked(shape, place):
    return pl.BlockSpec((1,) + shape[1:], lambda *_: (place,) + (0,) * (len(shape) - 1))


def cost(flops):
    return pl.CostEstimate(flops=flops, bytes_accessed=100_000, transcendentals=0)


PARAMS = pltpu.CompilerParams(vmem_limit_bytes=VMEM)
BLOCK = (CHUNK, C, SITES)
FULL = (ROUNDS, C, SITES)
WORK = [pltpu.VMEM(BLOCK, jnp.float32), pltpu.VMEM((CHUNK * C, 2 * SITES), jnp.bfloat16)]


def rounds_pass(part, inputs):
    state, events, embed, gains, taps, mixers, matrix = inputs
    first = part * CHUNK
    last = first + CHUNK
    outs = [BLOCK, BLOCK]
    return pl.pallas_call(
        functools.partial(rounds_kernel, first),
        grid=(1,),
        in_specs=[pl.BlockSpec(memory_space=pltpu.HBM)] * 7,
        out_specs=[whole(o) for o in outs],
        out_shape=[jax.ShapeDtypeStruct(o, jnp.float32) for o in outs],
        scratch_shapes=[
            pltpu.VMEM((HIST + last, C, SITES), jnp.float32),
            pltpu.VMEM((last, C, SITES), jnp.float32),
            pltpu.VMEM(events.shape, jnp.int32),
            pltpu.VMEM(embed.shape, jnp.float32),
            pltpu.VMEM(gains.shape, jnp.float32),
            pltpu.VMEM(taps.shape, jnp.float32),
            pltpu.VMEM((1,) + mixers.shape[1:], jnp.float32),
            pltpu.VMEM(matrix.shape, jnp.bfloat16),
        ]
        + WORK
        + [pltpu.SemaphoreType.DMA((last + 6,))],
        compiler_params=PARAMS,
        cost_estimate=cost(20_000_000),
    )(*inputs)


def tap_tables(kinds, taps, after):
    taps, after = lax.optimization_barrier((taps, after))
    outs = [jax.ShapeDtypeStruct((HALF + (kind == "far"), C, LANES), jnp.float32) for kind in kinds]
    return pl.pallas_call(
        functools.partial(tables_kernel, kinds),
        grid=(1,),
        in_specs=[whole(taps.shape[::-1])],
        out_specs=[whole(o.shape) for o in outs],
        out_shape=outs,
        compiler_params=PARAMS,
        cost_estimate=cost(1_000_000),
    )(taps.T)


def lattice_pass(axis, field, own, sides, gains, table, mixers, matrix):
    args = (field, own, *sides, gains, *table, mixers, matrix)
    return pl.pallas_call(
        functools.partial(lattice_kernel, axis, False, 0),
        grid=(1,),
        in_specs=[whole(a.shape) for a in args[:-2]] + [picked(mixers.shape, 1), whole(matrix.shape)],
        out_specs=[whole(BLOCK)] * 2,
        out_shape=[jax.ShapeDtypeStruct(BLOCK, jnp.float32)] * 2,
        scratch_shapes=WORK,
        compiler_params=PARAMS,
        cost_estimate=cost(1_200_000_000),
    )(*args)


def last_pass(axis, part, result, field, own, sides, gains, table, mixers, matrix):
    args = (field, own, *sides, gains, *table, mixers, matrix)
    specs = [whole(a.shape) for a in args[:-2]] + [picked(mixers.shape, 2), whole(matrix.shape)]
    aliases = {}
    if result is not None:
        aliases = {len(args): 0}
        args = args + (result,)
        specs = specs + [pl.BlockSpec(memory_space=pl.ANY)]
    return pl.pallas_call(
        functools.partial(lattice_kernel, axis, True, part),
        grid=(1,),
        in_specs=specs,
        out_specs=pl.BlockSpec(memory_space=pl.ANY),
        out_shape=jax.ShapeDtypeStruct(FULL, jnp.float32),
        scratch_shapes=WORK + [pltpu.SemaphoreType.DMA((CHUNK,))],
        input_output_aliases=aliases,
        compiler_params=PARAMS,
        cost_estimate=cost(1_200_000_000),
    )(*args)


def swap(own, axis, start):
    count = lax.axis_size(axis)
    pairs = [p for i in range(start, count - 1, 2) for p in ((i, i + 1), (i + 1, i))]
    return lax.ppermute(own, axis, pairs)


def local(state, events, event_embed, gains, taps_t, taps_y, taps_x, mixers):
    native, along_y, along_x = lane_orders()
    to_y = moving(native, along_y)
    to_x = moving(along_y, along_x)
    back = moving(along_x, native)
    inputs = [
        pltpu.with_memory_space_constraint(a, pltpu.HBM)
        for a in (state, events, event_embed[None, :], gains, taps_t.T, mixers, to_y)
    ]

    field_a, own_a = rounds_pass(0, inputs)
    odd_a = swap(own_a, "gy", 1)
    table_y, held = lax.optimization_barrier((tap_tables(("own", "far"), taps_y, own_a), own_a))
    even_a = swap(held, "gy", 0)
    field_b, own_b = rounds_pass(1, inputs)
    odd_b = swap(own_b, "gy", 1)
    even_b = swap(own_b, "gy", 0)
    field_a, own_a = lattice_pass("gy", field_a, own_a, (odd_a, even_a), gains, table_y, mixers, to_x)
    odd_a = swap(own_a, "gx", 1)
    near_x, held = lax.optimization_barrier((tap_tables(("own",), taps_x, own_a), own_a))
    even_a = swap(held, "gx", 0)
    field_b, own_b = lattice_pass("gy", field_b, own_b, (odd_b, even_b), gains, table_y, mixers, to_x)
    odd_b = swap(own_b, "gx", 1)
    far_x, held = lax.optimization_barrier((tap_tables(("far",), taps_x, own_b), own_b))
    even_b = swap(held, "gx", 0)
    table_x = (*near_x, *far_x)
    result = last_pass("gx", 0, None, field_a, own_a, (odd_a, even_a), gains, table_x, mixers, back)
    return last_pass("gx", 1, result, field_b, own_b, (odd_b, even_b), gains, table_x, mixers, back)


def solution(mesh):
    placed = (P(None, None, ("gx", "gy")), P(None, ("gx", "gy")), P(), P(), P(), P(), P(), P())
    return jax.shard_map(
        local, mesh=mesh, in_specs=placed, out_specs=P(None, None, ("gx", "gy")), check_vma=False
    )
```

```python
import functools

import jax
import jax.numpy as jnp
import numpy as np
from jax import lax
from jax.experimental import pallas as pl
from jax.experimental.pallas import tpu as pltpu
from jax.sharding import PartitionSpec as P

C = 96
ROUNDS = 12
SITES = 256
LANES = 128
HALF = 16
HIST = 8
KT = 9
CHUNK = 6
VMEM = 20 * 1024 * 1024


def lane_orders():
    x, y = np.divmod(np.arange(SITES), 16)
    native = x * 16 + y
    along_y = (x // 8) * 128 + y * 8 + x % 8
    along_x = (y // 8) * 128 + x * 8 + y % 8
    return native, along_y, along_x


def moving(source, target):
    matrix = np.zeros((SITES, SITES), np.float32)
    matrix[source, target] = 1.0
    return jnp.asarray(np.concatenate([matrix, matrix], axis=0), jnp.bfloat16)


def halves(value):
    high = value.astype(jnp.bfloat16)
    low = (value - high.astype(jnp.float32)).astype(jnp.bfloat16)
    return high, low


def dot(a, b):
    return jnp.dot(a, b, preferred_element_type=jnp.float32)


def columns(*rows):
    have = sum(r.shape[0] for r in rows)
    pad = -have % 8
    parts = list(rows) + ([jnp.zeros((pad, C), jnp.float32)] if pad else [])
    stacked = jnp.concatenate(parts, axis=0) if len(parts) > 1 else parts[0]
    stacked = jnp.concatenate([stacked, jnp.zeros((have + pad, LANES - C), jnp.float32)], axis=1)
    return jnp.transpose(stacked)


def spread(column, lanes):
    return jnp.broadcast_to(column, (column.shape[0], lanes))


def normed(field, gain):
    meansq = jnp.sum(field * field, axis=0, keepdims=True) * (1.0 / C)
    return field * lax.rsqrt(meansq + 1e-06) * gain


def tail(count, first, field, conv, mixers, matrix, gain, parts, field_out, next_out, sent=None):
    weights = jnp.concatenate([mixers[0, 0], mixers[0, 1]], axis=0) * 0.5
    weights_high, weights_low = halves(weights)
    weights_twice = jnp.concatenate([weights_high, weights_high], axis=1)
    for r in range(count):
        high, low = halves(conv[r])
        both = dot(weights_twice, jnp.concatenate([high, low], axis=0)) + dot(weights_low, high)
        value = both[:C]
        mixed = field[first + r] + value + value * jnp.tanh(both[C:])
        high, low = halves(mixed)
        rows = slice(r * C, (r + 1) * C)
        parts[rows, :SITES] = high
        parts[rows, SITES:] = low
    moved = dot(parts[...], matrix[...])
    for r in range(count):
        here = moved[r * C : (r + 1) * C]
        field_out[r // CHUNK][r % CHUNK] = here
        if sent is not None:
            sent(r)
        if next_out is not None:
            next_out[r // CHUNK][r % CHUNK] = normed(here, gain)


def rounds_kernel(
    first, state_in, events_in, embed_in, gains_in, taps_in, mixers_in, matrix_in, *refs
):
    outs, work = refs[: 2 * PARTS], refs[2 * PARTS :]
    ext, state, events, embed, gains, taps, mixers, matrix, conv, parts, sems = work
    last = state.shape[0]
    count = last - first
    small = [
        (gains_in, gains),
        (taps_in, taps),
        (embed_in, embed),
        (events_in, events),
        (mixers_in.at[0:1], mixers),
        (matrix_in, matrix),
    ]
    rounds = range(max(0, first - HIST), last)
    copies = [pltpu.make_async_copy(a, b, sems.at[last + n]) for n, (a, b) in enumerate(small)]
    loads = {r: pltpu.make_async_copy(state_in.at[r], state.at[r], sems.at[r]) for r in rounds}
    for copy in copies[:4] + list(loads.values()) + copies[4:]:
        copy.start()
    for copy in copies[:4]:
        copy.wait()
    cols = columns(taps[...], gains[...], embed[...])[:C]
    gain_now = spread(cols[:, KT : KT + 1], SITES)
    gain_next = spread(cols[:, KT + 1 : KT + 2], SITES)
    embed_here = spread(cols[:, KT + 3 : KT + 4], SITES)
    for s in range(first, HIST):
        past = 2.0 * events[s : s + 1, :].astype(jnp.float32) - 1.0
        ext[s] = embed_here * past
    for r in rounds:
        loads[r].wait()
        ext[HIST + r] = normed(state[r], gain_now)
    for i in range(C // 8):
        rows = slice(i * 8, (i + 1) * 8)
        tap = [spread(cols[rows, k : k + 1], LANES) for k in range(KT)]
        for half in range(2):
            lanes = slice(half * LANES, (half + 1) * LANES)
            seen = [ext[first + s, rows, lanes] for s in range(count + KT - 1)]
            for r in range(count):
                total = tap[0] * seen[r]
                for k in range(1, KT):
                    total = total + tap[k] * seen[r + k]
                conv[r, rows, lanes] = total
    for copy in copies[4:]:
        copy.wait()
    tail(count, first, state, conv, mixers, matrix, gain_next, parts, outs[0::2], outs[1::2])


def tables_kernel(kinds, taps, *tables):
    lane_place = lax.broadcasted_iota(jnp.int32, (8, LANES), 1) // 8
    cols = columns(taps[...])[:C]
    for i in range(C // 8):
        rows = slice(i * 8, (i + 1) * 8)
        tap = [spread(cols[rows, k : k + 1], LANES) for k in range(2 * HALF + 1)]
        for kind, table in zip(kinds, tables):
            for d in range(HALF):
                keep = turned_place(lane_place, d) >= d
                if kind == "own":
                    table[d, rows, :] = jnp.where(keep, tap[d + HALF], tap[d])
                else:
                    table[d, rows, :] = jnp.where(keep, tap[d], tap[d + HALF])
            if kind == "far":
                table[HALF, rows, :] = tap[2 * HALF]


def turned_place(lane_place, d):
    return (lane_place + 1) & (HALF - 1) if d % 2 else lane_place


def lattice_kernel(axis, ends, part, *refs):
    field, own, odd, even, gains, tap_own, tap_far, mixers, matrix = refs[:9]
    if ends:
        result, conv, parts, sems = refs[-4:]
    else:
        field_out, next_out, conv, parts = refs[9:]
        gain = spread(columns(gains[...])[:C, 2:3], SITES)
    count = field.shape[0]
    lane_place = lax.broadcasted_iota(jnp.int32, (8, LANES), 1) // 8
    first_of_pair = lax.rem(lax.axis_index(axis), 2) == 0

    def conv_tile(i, carry):
        rows = pl.ds(pl.multiple_of(i * 8, 8), 8)
        for r0 in range(0, count, 2):
            spots = [
                (r, slice(half * LANES, (half + 1) * LANES)) for r in range(r0, r0 + 2) for half in range(2)
            ]
            here = [own[r, rows, lanes] for r, lanes in spots]
            one = [even[r, rows, lanes] for r, lanes in spots]
            two = [odd[r, rows, lanes] for r, lanes in spots]
            low = [jnp.where(first_of_pair, b, a) for a, b in zip(one, two)]
            high = [jnp.where(first_of_pair, a, b) for a, b in zip(one, two)]
            turned = [[pltpu.roll(v, LANES - 8, 1) for v in vs] for vs in (here, low, high)]
            sides = ((here, low, high), turned)
            totals = [tap_far[HALF, rows, :] * high[n] for n in range(len(spots))]
            for d in range(0, HALF, 2):
                sums = [None] * len(spots)
                for e in (d, d + 1):
                    near = tap_own[e, rows, :]
                    far = tap_far[e, rows, :]
                    keep = turned_place(lane_place, e) >= e
                    mine, under, over = sides[e - d]
                    for n in range(len(spots)):
                        other = jnp.where(keep, under[n], over[n]) if e else under[n]
                        piece = near * mine[n] + far * other
                        sums[n] = piece if e == d else sums[n] + piece
                for n in range(len(spots)):
                    totals[n] = totals[n] + (pltpu.roll(sums[n], LANES - 8 * d, 1) if d else sums[n])
            for n, (r, lanes) in enumerate(spots):
                conv[r, rows, lanes] = totals[n]
        return carry

    lax.fori_loop(0, C // 8, conv_tile, 0)
    if not ends:
        tail(count, 0, field, conv, mixers, matrix, gain, parts, [field_out], [next_out])
        return

    copies = [
        pltpu.make_async_copy(conv.at[r], result.at[part * CHUNK + r], sems.at[r]) for r in range(count)
    ]
    tail(count, 0, field, conv, mixers, matrix, None, parts, [conv], None, lambda r: copies[r].start())
    for copy in copies:
        copy.wait()


def whole(shape):
    return pl.BlockSpec(shape, lambda *_: (0,) * len(shape))


def picked(shape, place):
    return pl.BlockSpec((1,) + shape[1:], lambda *_: (place,) + (0,) * (len(shape) - 1))


def cost(flops):
    return pl.CostEstimate(flops=flops, bytes_accessed=100_000, transcendentals=0)


PARAMS = pltpu.CompilerParams(vmem_limit_bytes=VMEM)
BLOCK = (CHUNK, C, SITES)
PARTS = ROUNDS // CHUNK
FULL = (ROUNDS, C, SITES)
WORK = [pltpu.VMEM(BLOCK, jnp.float32), pltpu.VMEM((CHUNK * C, 2 * SITES), jnp.bfloat16)]


def rounds_pass(inputs):
    state, events, embed, gains, taps, mixers, matrix = inputs
    first, last = 0, ROUNDS
    outs = [BLOCK, BLOCK] * PARTS
    return pl.pallas_call(
        functools.partial(rounds_kernel, first),
        grid=(1,),
        in_specs=[pl.BlockSpec(memory_space=pltpu.HBM)] * 7,
        out_specs=[whole(o) for o in outs],
        out_shape=[jax.ShapeDtypeStruct(o, jnp.float32) for o in outs],
        scratch_shapes=[
            pltpu.VMEM((HIST + last, C, SITES), jnp.float32),
            pltpu.VMEM((last, C, SITES), jnp.float32),
            pltpu.VMEM(events.shape, jnp.int32),
            pltpu.VMEM(embed.shape, jnp.float32),
            pltpu.VMEM(gains.shape, jnp.float32),
            pltpu.VMEM(taps.shape, jnp.float32),
            pltpu.VMEM((1,) + mixers.shape[1:], jnp.float32),
            pltpu.VMEM(matrix.shape, jnp.bfloat16),
        ]
        + [pltpu.VMEM(FULL, jnp.float32), pltpu.VMEM((ROUNDS * C, 2 * SITES), jnp.bfloat16)]
        + [pltpu.SemaphoreType.DMA((last + 6,))],
        compiler_params=PARAMS,
        cost_estimate=cost(20_000_000),
    )(*inputs)


def tap_tables(kinds, taps, after):
    taps, after = lax.optimization_barrier((taps, after))
    outs = [jax.ShapeDtypeStruct((HALF + (kind == "far"), C, LANES), jnp.float32) for kind in kinds]
    return pl.pallas_call(
        functools.partial(tables_kernel, kinds),
        grid=(1,),
        in_specs=[whole(taps.shape[::-1])],
        out_specs=[whole(o.shape) for o in outs],
        out_shape=outs,
        compiler_params=PARAMS,
        cost_estimate=cost(1_000_000),
    )(taps.T)


def lattice_pass(axis, field, own, sides, gains, table, mixers, matrix):
    args = (field, own, *sides, gains, *table, mixers, matrix)
    return pl.pallas_call(
        functools.partial(lattice_kernel, axis, False, 0),
        grid=(1,),
        in_specs=[whole(a.shape) for a in args[:-2]] + [picked(mixers.shape, 1), whole(matrix.shape)],
        out_specs=[whole(BLOCK)] * 2,
        out_shape=[jax.ShapeDtypeStruct(BLOCK, jnp.float32)] * 2,
        scratch_shapes=WORK,
        compiler_params=PARAMS,
        cost_estimate=cost(1_200_000_000),
    )(*args)


def last_pass(axis, part, result, field, own, sides, gains, table, mixers, matrix):
    args = (field, own, *sides, gains, *table, mixers, matrix)
    specs = [whole(a.shape) for a in args[:-2]] + [picked(mixers.shape, 2), whole(matrix.shape)]
    aliases = {}
    if result is not None:
        aliases = {len(args): 0}
        args = args + (result,)
        specs = specs + [pl.BlockSpec(memory_space=pl.ANY)]
    return pl.pallas_call(
        functools.partial(lattice_kernel, axis, True, part),
        grid=(1,),
        in_specs=specs,
        out_specs=pl.BlockSpec(memory_space=pl.ANY),
        out_shape=jax.ShapeDtypeStruct(FULL, jnp.float32),
        scratch_shapes=WORK + [pltpu.SemaphoreType.DMA((CHUNK,))],
        input_output_aliases=aliases,
        compiler_params=PARAMS,
        cost_estimate=cost(1_200_000_000),
    )(*args)


def swap(own, axis, start):
    count = lax.axis_size(axis)
    pairs = [p for i in range(start, count - 1, 2) for p in ((i, i + 1), (i + 1, i))]
    return lax.ppermute(own, axis, pairs)


def local(state, events, event_embed, gains, taps_t, taps_y, taps_x, mixers):
    native, along_y, along_x = lane_orders()
    to_y = moving(native, along_y)
    to_x = moving(along_y, along_x)
    back = moving(along_x, native)
    inputs = [
        pltpu.with_memory_space_constraint(a, pltpu.HBM)
        for a in (state, events, event_embed[None, :], gains, taps_t.T, mixers, to_y)
    ]

    field_a, own_a, field_b, own_b = rounds_pass(inputs)
    odd_a = swap(own_a, "gy", 1)
    table_y, held = lax.optimization_barrier((tap_tables(("own", "far"), taps_y, own_a), own_a))
    even_a = swap(held, "gy", 0)
    odd_b = swap(own_b, "gy", 1)
    even_b = swap(own_b, "gy", 0)
    field_a, own_a = lattice_pass("gy", field_a, own_a, (odd_a, even_a), gains, table_y, mixers, to_x)
    odd_a = swap(own_a, "gx", 1)
    near_x, held = lax.optimization_barrier((tap_tables(("own",), taps_x, own_a), own_a))
    even_a = swap(held, "gx", 0)
    field_b, own_b = lattice_pass("gy", field_b, own_b, (odd_b, even_b), gains, table_y, mixers, to_x)
    odd_b = swap(own_b, "gx", 1)
    far_x, held = lax.optimization_barrier((tap_tables(("far",), taps_x, own_b), own_b))
    even_b = swap(held, "gx", 0)
    table_x = (*near_x, *far_x)
    result = last_pass("gx", 0, None, field_a, own_a, (odd_a, even_a), gains, table_x, mixers, back)
    return last_pass("gx", 1, result, field_b, own_b, (odd_b, even_b), gains, table_x, mixers, back)


def solution(mesh):
    placed = (P(None, None, ("gx", "gy")), P(None, ("gx", "gy")), P(), P(), P(), P(), P(), P())
    return jax.shard_map(
        local, mesh=mesh, in_specs=placed, out_specs=P(None, None, ("gx", "gy")), check_vma=False
    )
```
